256 devices in a mesh: fsdp: 64 (over x, z, core), tp: 4 (over y).
Axes of the slice: x: 4, y: 4, z: 8, core: 2. Of those that a mesh axis runs over, the one named last changes fastest.
Arguments:
- momentum: bfloat16 [40960, 16384], P('fsdp', 'tp'), may hold values from -100 to 100, as said below
- basis: bfloat16 [16384, 256], P(('tp', 'fsdp')), may hold values from -6 to 6
Outputs:
- momentum_new: bfloat16 [40960, 16384], P('fsdp', 'tp')
- basis_new: float32 [16384, 256], P(('tp', 'fsdp'))
The draws below stay inside these ranges and needn't reach their ends.
Inputs may be any that keep to these rules, and one draw needn't show every extreme that they name: momentum entries are real-valued and full rank.
All inputs are finite; a program needn't handle non-finite values.
Results may differ from the reference program's by a relative error of at most 0.0016.
Values may be sent and summed in bfloat16 or wider, within the bound.
No kernel may reach another device: no remote copies, remote signals or barrier semaphores. Data moves between devices by JAX's collectives and lax.ppermute only.
A program may use at most 128 MiB of HBM per device.

```python
import math
import jax
import jax.numpy as jnp
from jax import lax

D = 16384
R = 256
ROW_DEV = 640
ROWS = 40960
N_FSDP = 64


def draw_momentum(key, part):
    key = jax.random.fold_in(key, 11)
    subkeys = jax.random.split(key, 6)
    group_of = jax.random.permutation(subkeys[5], D) % R
    level = jnp.arange(R, dtype=jnp.float32)
    noise_part = jax.random.truncated_normal(subkeys[0], -4.0, 4.0, (ROWS, D), jnp.float32)
    left_block = jax.random.truncated_normal(subkeys[1], -2.5, 2.5, (ROWS, R), jnp.float32)
    strengths = 3.0 * jnp.exp(-2.5 * level / R)
    right_vec = jax.random.uniform(subkeys[2], (1, D), jnp.float32, -1.5, 1.5)
    row_scale = jnp.exp(jax.random.uniform(subkeys[3], (ROWS, 1), jnp.float32, math.log(0.5), math.log(2.0)))
    col_scale = jnp.exp(jax.random.uniform(subkeys[4], (1, D), jnp.float32, math.log(0.32), math.log(3.2)))
    spread_part = jnp.take(left_block * strengths[None, :], group_of, axis=1)
    return (row_scale * col_scale * (noise_part + spread_part * right_vec)).astype(jnp.bfloat16)


def block_levels(rng, dims, shards, smallest, high):
    factor_of, own = 1.0, jax.random.fold_in(rng, 6)
    for dim, shards_of in shards:
        steps = jnp.exp(jax.random.uniform(jax.random.fold_in(own, dim), (shards_of,), jnp.float32, smallest / len(shards), high / len(shards)))
        factor_of = factor_of * jnp.repeat(steps, dims[dim] // shards_of).reshape([-1 if axis == dim else 1 for axis in range(len(dims))])
    return factor_of


def bell_draw(rng, dims, deviation, most, pieces=(), kind=jnp.bfloat16):
    drawn = deviation * jax.random.normal(rng, dims, jnp.float32)
    if pieces:
        drawn = drawn * block_levels(rng, dims, pieces, -0.22, 0.18)
    return jnp.clip(drawn, -most, most).astype(kind)


def setup_inputs(seed: int = 0) -> dict:
    streams_of = jax.random.split(jax.random.key(seed), 3)
    return {
        "momentum": draw_momentum(jax.random.fold_in(streams_of[2], 71), 0),
        "basis": bell_draw(streams_of[1], (D, R), 1.0, 6.0, ((0, 256),)),
    }


feedback_rate = 0.05
norm_eps = 1e-06

def reference(momentum, basis):
    panel_full = jnp.dot(momentum.astype(jnp.float32), basis.astype(jnp.float32), preferred_element_type=jnp.float32)
    q_factor, r_factor = jnp.linalg.qr(panel_full)
    diag_signs = jnp.sign(jnp.diagonal(r_factor))
    orthonormal = (q_factor * diag_signs[None, :]).astype(jnp.bfloat16)
    project = lax.dot_general(momentum.astype(jnp.float32), orthonormal.astype(jnp.float32), (((0,), (0,)), ((), ())), preferred_element_type=jnp.float32)
    basis_new = project * lax.rsqrt(lax.optimization_barrier(jnp.mean(project * project, axis=0, keepdims=True)) + norm_eps)
    lowrank = project.astype(jnp.bfloat16)

    def refresh(paired):
        rows_now, ortho_now = paired
        update = lax.dot_general(ortho_now.astype(jnp.float32), lowrank.astype(jnp.float32), (((1,), (1,)), ((), ())), preferred_element_type=jnp.float32)
        return (rows_now.astype(jnp.float32) - feedback_rate * update).astype(jnp.bfloat16)
    blocked = lax.map(refresh, (momentum.reshape(N_FSDP, ROW_DEV, D), orthonormal.reshape(N_FSDP, ROW_DEV, R)))
    return (blocked.reshape(ROWS, D), basis_new)
```

```python
import functools

import jax
import jax.numpy as jnp
from jax import lax
from jax.experimental import pallas as pl
from jax.experimental.pallas import tpu as pltpu
from jax.sharding import Mesh
from jax.sharding import PartitionSpec as P

feedback_rate = 0.05
norm_eps = 1e-06
highest = lax.Precision.HIGHEST
f32 = jnp.float32
bf16 = jnp.bfloat16

NX, NZ, NC, NY = 4, 8, 2, 4
WIDE = 128
BLOCK = 64
PIECES = 2
ORDERS = ((1, 2, 0, 3), (3, 2, 0, 1))


def vmem():
    return pl.BlockSpec(memory_space=pltpu.VMEM)


def smem():
    return pl.BlockSpec(memory_space=pltpu.SMEM)


def params(mib=16):
    return pltpu.CompilerParams(vmem_limit_bytes=mib << 20)


def cost(us):
    return pl.CostEstimate(flops=int(us * 1.15e9), bytes_accessed=0, transcendentals=0)


def swap(value, axis):
    return lax.all_to_all(value, axis, 0, 0, tiled=True)


def other_core(value):
    return lax.ppermute(value, "core", [(0, 1), (1, 0)])


def flip(value, axis, bit):
    return lax.ppermute(value, axis, [(i, i ^ bit) for i in range(lax.axis_size(axis))])


def gather_chip(copies, beside):
    line = swap(copies, "z")
    near, across, far = flip(line, "x", 1), flip(line, "x", 3), flip(line, "x", 2)
    line, given = beside(line)
    near, given = lax.optimization_barrier((near, given))
    mine = [line, near, far, across]
    return mine, [other_core(part) for part in mine], given


def stage_kernel(momentum, out, sems):
    rows = momentum.shape[0] // sems.shape[0]
    copies = []
    for i in range(sems.shape[0]):
        at = pl.ds(i * rows, rows)
        copies.append(pltpu.make_async_copy(momentum.at[at, :], out.at[at, :], sems.at[i]))
        copies[-1].start()
    for copy in copies:
        copy.wait()


def stage_call(momentum):
    staged = pl.pallas_call(
        stage_kernel,
        in_specs=[pl.BlockSpec(memory_space=pl.ANY)],
        out_specs=vmem(),
        out_shape=pltpu.VMEM(momentum.shape, momentum.dtype),
        scratch_shapes=[pltpu.SemaphoreType.DMA((4,))],
        compiler_params=params(),
        cost_estimate=cost(2.5),
        name="stage",
    )(pltpu.with_memory_space_constraint(momentum, pltpu.HBM))
    return pltpu.with_memory_space_constraint(staged, pltpu.VMEM)


def panel_kernel(idx, momentum, *refs):
    mine, other = refs[:NX], refs[NX : 2 * NX]
    outs, (right, total) = refs[2 * NX : 2 * NX + NY], refs[2 * NX + NY :]
    x, c, y = idx[0], idx[2], idx[3]
    half = WIDE // NC
    piece = NZ * WIDE
    for s in range(NX):
        for t in range(NZ):
            at = (x ^ s) * piece + t * WIDE
            right[pl.ds(pl.multiple_of(at + c * half, half), half), :] = mine[s][t]
            right[pl.ds(pl.multiple_of(at + (1 - c) * half, half), half), :] = other[s][t]
    for s in range(NX):
        at = slice(s * piece, (s + 1) * piece)
        part = jnp.dot(momentum[:, at], right[at, :], preferred_element_type=f32)
        total[...] = part if s == 0 else total[...] + part
    rows = total.shape[0] // NY
    for s in range(NY):
        outs[s][...] = total[pl.ds(pl.multiple_of((y ^ s) * rows, 8), rows), :]


def panel_call(idx, momentum, mine, other):
    rows, cols = momentum.shape
    rank = mine[0].shape[-1]
    return pl.pallas_call(
        panel_kernel,
        in_specs=[smem()] + [vmem()] * (1 + 2 * NX),
        out_specs=[vmem()] * NY,
        out_shape=[jax.ShapeDtypeStruct((rows // NY, rank), f32)] * NY,
        scratch_shapes=[pltpu.VMEM((cols, rank), bf16), pltpu.VMEM((rows, rank), f32)],
        compiler_params=params(),
        cost_estimate=cost(3.5),
        name="panel",
    )(idx, momentum, *mine, *other)


def tally_kernel(*refs):
    refs[-1][...] = (refs[0][...] + refs[1][...]) + (refs[2][...] + refs[3][...])


def tally_call(parts):
    return pl.pallas_call(
        tally_kernel,
        in_specs=[vmem()] * len(parts),
        out_specs=vmem(),
        out_shape=jax.ShapeDtypeStruct(parts[0].shape, f32),
        compiler_params=params(),
        cost_estimate=cost(0.7),
        name="tally",
    )(*parts)


def fold_kernel(pieces, out):
    got = pieces[0]
    for i in range(1, pieces.shape[0]):
        got = got + pieces[i]
    out[...] = got


def fold_call(pieces):
    return pl.pallas_call(
        fold_kernel,
        in_specs=[vmem()],
        out_specs=vmem(),
        out_shape=jax.ShapeDtypeStruct(pieces.shape[1:], f32),
        compiler_params=params(),
        cost_estimate=cost(0.8),
        name="fold",
    )(pieces)


def prep_kernel(idx, *refs):
    parts = refs[:NY]
    panel, pieces, gram, across = refs[NY:]
    y = idx[3]
    rows = parts[0].shape[0]
    for s in range(NY):
        panel[pl.ds(pl.multiple_of((y ^ s) * rows, 8), rows), :] = parts[s][...]
    whole = panel[...]
    turned = whole.T
    rank = turned.shape[0]
    across[...] = turned
    own = across[pl.ds(pl.multiple_of(y * (rank // NY), rank // NY), rank // NY), :]
    gram[...] = jnp.dot(own, whole, precision=highest, preferred_element_type=f32)
    for i in range(PIECES):
        now = turned.astype(bf16)
        pieces[i * rank : (i + 1) * rank, :] = now
        turned = turned - now.astype(f32)


def prep_call(idx, parts):
    rows, rank = parts[0].shape[0] * NY, parts[0].shape[1]
    return pl.pallas_call(
        prep_kernel,
        in_specs=[smem()] + [vmem()] * NY,
        out_specs=[vmem()] * 3,
        out_shape=[
            jax.ShapeDtypeStruct((rows, rank), f32),
            jax.ShapeDtypeStruct((PIECES * rank, rows), bf16),
            jax.ShapeDtypeStruct((rank // NY, rank), f32),
        ],
        scratch_shapes=[pltpu.VMEM((rank, rows), f32)],
        compiler_params=params(),
        cost_estimate=cost(1.5),
        name="prep",
    )(idx, *parts)


def project_kernel(part, idx, momentum, pieces, keep, send):
    x, c = idx[0], idx[2]
    rank = pieces.shape[0] // PIECES
    low = rank // 2
    first = c == 0
    wide = 2 * WIDE
    for i, s in enumerate(ORDERS[part]):
        for j in range(0, NZ // 2 * WIDE, wide):
            at = pl.multiple_of(((x ^ s) * 2 + part) * (NZ // 2 * WIDE) + j, wide)
            got = jnp.dot(pieces[...], momentum[:, pl.ds(at, wide)], preferred_element_type=f32)
            got = got[rank:] + got[:rank]
            for k in range(2):
                here = got[:, k * WIDE : (k + 1) * WIDE]
                top, bottom = here[:low], here[low:]
                keep[i, j // WIDE + k] = jnp.where(first, top, bottom)
                send[i, j // WIDE + k] = jnp.where(first, bottom, top)


def project_call(idx, momentum, pieces, part):
    rank = pieces.shape[0] // PIECES
    shape = jax.ShapeDtypeStruct((NX, NZ // 2, rank // 2, WIDE), f32)
    return pl.pallas_call(
        functools.partial(project_kernel, part),
        in_specs=[smem(), vmem(), vmem()],
        out_specs=[vmem()] * 2,
        out_shape=[shape] * 2,
        compiler_params=params(),
        cost_estimate=cost(3.5),
        name=f"project{part}",
    )(idx, momentum, pieces)


def first_kernel(keep, got, near, rest):
    for s in range(2):
        near[s] = keep[s] + got[s]
        rest[s] = keep[2 + s] + got[2 + s]


def first_call(keep, got):
    return pl.pallas_call(
        first_kernel,
        in_specs=[vmem()] * 2,
        out_specs=[vmem()] * 2,
        out_shape=[jax.ShapeDtypeStruct((2, *keep.shape[1:]), f32)] * 2,
        compiler_params=params(),
        cost_estimate=cost(0.9),
        name="first",
    )(keep, got)


def second_kernel(rest, near, own, away):
    own[...] = rest[0] + near[0]
    away[...] = rest[1] + near[1]


def second_call(rest, near):
    return pl.pallas_call(
        second_kernel,
        in_specs=[vmem()] * 2,
        out_specs=[vmem()] * 2,
        out_shape=[jax.ShapeDtypeStruct(rest.shape[1:], f32)] * 2,
        compiler_params=params(),
        cost_estimate=cost(0.9),
        name="second",
    )(rest, near)


def line_kernel(own0, near0, own1, near1, out):
    deep = own0.shape[0]
    out[:deep] = own0[...] + near0[...]
    out[deep:] = own1[...] + near1[...]


def line_call(parts):
    deep, low, wide = parts[0].shape
    return pl.pallas_call(
        line_kernel,
        in_specs=[vmem()] * len(parts),
        out_specs=vmem(),
        out_shape=jax.ShapeDtypeStruct((2 * deep, low, wide), f32),
        compiler_params=params(),
        cost_estimate=cost(0.8),
        name="line",
    )(*parts)


def share_kernel(idx, mine, other, solver, low_rank, share, turned):
    c = idx[2]
    first = c == 0
    top = jnp.where(first, mine[...], other[...])
    bottom = jnp.where(first, other[...], mine[...])
    whole = jnp.concatenate([top, bottom], axis=0)
    got = jnp.dot(solver[...], whole, precision=highest, preferred_element_type=f32)
    low = got.shape[0] // 2
    rounded = jnp.where(first, got[:low], got[low:]).astype(bf16)
    for t in range(NZ):
        low_rank[t] = rounded
    turned[...] = got.T
    half = WIDE // NC
    share[...] = turned[pl.ds(pl.multiple_of(c * half, half), half), :]


def share_call(idx, mine, other, solver):
    low, wide = mine.shape
    rank = 2 * low
    return pl.pallas_call(
        share_kernel,
        in_specs=[smem()] + [vmem()] * 3,
        out_specs=[vmem()] * 2,
        out_shape=[
            jax.ShapeDtypeStruct((NZ, low, wide), bf16),
            jax.ShapeDtypeStruct((wide // NC, rank), f32),
        ],
        scratch_shapes=[pltpu.VMEM((wide, rank), f32)],
        compiler_params=params(),
        cost_estimate=cost(1.0),
        name="share",
    )(idx, mine, other, solver)


def ortho_kernel(panel, solver, ortho):
    across = (((1,), (1,)), ((), ()))
    ortho[...] = lax.dot_general(
        panel[...], solver[...], across, precision=highest, preferred_element_type=f32
    ).astype(bf16)


def ortho_call(panel, solver):
    rows, rank = panel.shape
    return pl.pallas_call(
        ortho_kernel,
        in_specs=[vmem()] * 2,
        out_specs=vmem(),
        out_shape=jax.ShapeDtypeStruct((rows, rank), bf16),
        compiler_params=params(),
        cost_estimate=cost(0.7),
        name="ortho",
    )(panel, solver)


def square_kernel(idx, *refs):
    mine, other, out = refs[:NX], refs[NX : 2 * NX], refs[-1]
    c = idx[2]

    def total(group):
        acc = None
        for ref in group:
            for t in range(NZ):
                v = ref[t].astype(f32)
                acc = v * v if acc is None else acc + v * v
        return jnp.sum(acc, axis=1, keepdims=True)

    a, b = total(mine), total(other)
    first = c == 0
    whole = jnp.concatenate([jnp.where(first, a, b), jnp.where(first, b, a)], axis=0)
    out[...] = jnp.broadcast_to(whole, (whole.shape[0], WIDE)).T[:8]


def square_call(idx, mine, other):
    low = mine[0].shape[1]
    return pl.pallas_call(
        square_kernel,
        in_specs=[smem()] + [vmem()] * (2 * NX),
        out_specs=vmem(),
        out_shape=jax.ShapeDtypeStruct((8, 2 * low), f32),
        compiler_params=params(),
        cost_estimate=cost(1.0),
        name="square",
    )(idx, *mine, *other)


def update_kernel(idx, momentum, ortho, *refs):
    mine, other = refs[:NX], refs[NX : 2 * NX]
    out, fresh, right, sems = refs[2 * NX :]
    x, c = idx[0], idx[2]
    piece = NZ * WIDE
    low = right.shape[0] // 2
    for s in range(NX):
        for t in range(NZ):
            at = pl.ds(pl.multiple_of((x ^ s) * piece + t * WIDE, WIDE), WIDE)
            right[pl.ds(pl.multiple_of(c * low, low), low), at] = mine[s][t]
            right[pl.ds(pl.multiple_of((1 - c) * low, low), low), at] = other[s][t]
    outward = []
    for s in range(NX):
        for j in range(s * piece, (s + 1) * piece, 2 * WIDE):
            at = slice(j, j + 2 * WIDE)
            got = jnp.dot(ortho[...], right[:, at], preferred_element_type=f32)
            fresh[:, at] = (momentum[:, at].astype(f32) - feedback_rate * got).astype(bf16)
        at = pl.ds(s * piece, piece)
        outward.append(pltpu.make_async_copy(fresh.at[:, at], out.at[:, at], sems.at[s]))
        outward[-1].start()
    for copy in outward:
        copy.wait()


def update_call(idx, momentum, ortho, mine, other):
    rows, cols = momentum.shape
    rank = ortho.shape[1]
    return pl.pallas_call(
        update_kernel,
        in_specs=[smem()] + [vmem()] * (2 + 2 * NX),
        out_specs=pl.BlockSpec(memory_space=pl.ANY),
        out_shape=jax.ShapeDtypeStruct((rows, cols), bf16),
        scratch_shapes=[
            pltpu.VMEM((rows, cols), bf16),
            pltpu.VMEM((rank, cols), bf16),
            pltpu.SemaphoreType.DMA((NX,)),
        ],
        compiler_params=params(),
        cost_estimate=cost(5.0),
        name="update",
    )(idx, momentum, ortho, *mine, *other)


def invert_block(block):
    size = block.shape[0]
    strips = size // 8
    row = lax.broadcasted_iota(jnp.int32, (8, 2 * size), 0)
    eye = (
        lax.broadcasted_iota(jnp.int32, (size, size), 0)
        == lax.broadcasted_iota(jnp.int32, (size, size), 1)
    ).astype(f32)
    both = jnp.concatenate([eye, block], axis=1)
    wide = [both[8 * t : 8 * t + 8] for t in range(strips)]
    shape = (8, 2 * size)
    done = []
    for s in range(strips):
        cols = {
            t: [jnp.broadcast_to(wide[t][:, size + 8 * s + j : size + 8 * s + j + 1], shape) for j in range(8)]
            for t in range(s, strips)
        }
        scale = jnp.ones(shape, f32)
        for k in range(8):
            over = lambda v: jnp.broadcast_to(v[k : k + 1], shape)
            pivot = over(cols[s][k])
            inverse = 1.0 / pivot
            scale = jnp.where(row == k, lax.rsqrt(pivot), scale)
            lead = over(wide[s])
            heads = {j: over(cols[s][j]) for j in range(k + 1, 8)}
            for t in range(s, strips):
                factor = cols[t][k] * inverse
                if t == s:
                    factor = jnp.where(row > k, factor, 0.0)
                wide[t] = wide[t] - factor * lead
                for j in range(k + 1, 8):
                    cols[t][j] = cols[t][j] - factor * heads[j]
        done.append(wide[s] * scale)
    return jnp.concatenate(done, axis=0)[:, :size]

def solver_kernel(idx, *refs):
    parts, (out, left, right) = refs[:NY], refs[NY:]
    y = idx[3]
    rank = out.shape[0]
    rows = rank // NY
    for s in range(NY):
        left[pl.ds(pl.multiple_of((y ^ s) * rows, 8), rows), :] = parts[s][...]
    right[...] = (
        lax.broadcasted_iota(jnp.int32, (rank, rank), 0)
        == lax.broadcasted_iota(jnp.int32, (rank, rank), 1)
    ).astype(f32)
    across = (((1,), (1,)), ((), ()))
    for at in range(0, rank, BLOCK):
        end = at + BLOCK
        inverse = invert_block(left[at:end, at:end])
        rows = jnp.dot(inverse, right[at:end, :end], precision=highest, preferred_element_type=f32)
        out[at:end, :end] = rows
        if end < rank:
            out[at:end, end:] = jnp.zeros((BLOCK, rank - end), f32)
            down = lax.dot_general(left[end:, at:end], inverse, across, precision=highest, preferred_element_type=f32)
            left[end:, end:] -= lax.dot_general(down, down, across, precision=highest, preferred_element_type=f32)
            right[end:, :end] -= jnp.dot(down, rows, precision=highest, preferred_element_type=f32)

def solver_call(idx, parts):
    rank = parts[0].shape[1]
    return pl.pallas_call(
        solver_kernel,
        in_specs=[smem()] + [vmem()] * NY,
        out_specs=vmem(),
        out_shape=jax.ShapeDtypeStruct((rank, rank), f32),
        scratch_shapes=[pltpu.VMEM((rank, rank), f32)] * 2,
        compiler_params=params(),
        cost_estimate=cost(9.4),
        name="solver",
    )(idx, *parts)


def on_device(momentum, basis):
    total_cols = momentum.shape[1] * NY
    rank = basis.shape[1]
    x, z, c, y = (lax.axis_index(axis) for axis in ("x", "z", "core", "y"))
    idx = jnp.stack([x, z, c, y] + [x ^ s for order in ORDERS for s in order]).astype(jnp.int32)

    after = lax.optimization_barrier

    def stage_beside(line):
        line, late = after((line, momentum))
        return line, stage_call(late)

    mine, other, staged = gather_chip(jnp.broadcast_to(basis[None], (NZ, *basis.shape)), stage_beside)
    parts = panel_call(idx, staged, mine, other)
    own = tally_call([parts[0]] + [flip(parts[s], "y", s) for s in (1, 3, 2)])
    panel, pieces, gram = prep_call(idx, [own] + [flip(own, "y", s) for s in (1, 2, 3)])

    keep0, send0 = project_call(idx, staged, pieces, 0)
    got0 = other_core(send0)
    gram = gram + other_core(gram)
    pieces, gram = after((pieces, gram))
    keep1, send1 = project_call(idx, staged, pieces, 1)
    got1 = other_core(send1)
    near0, rest0 = first_call(keep0, got0)
    near1, rest1 = first_call(keep1, got1)
    near0, near1 = flip(near0, "x", ORDERS[0][0]), flip(near1, "x", ORDERS[1][0])
    gram = tally_call([gram] + [flip(gram, "z", s) for s in (1, 2, 3)])
    rest0, gram = after((rest0, gram))
    own0, away0 = second_call(rest0, near0)
    away0 = flip(away0, "x", ORDERS[0][3])
    gram = gram + flip(gram, "z", 4)
    rest1, gram = after((rest1, gram))
    own1, away1 = second_call(rest1, near1)
    away1 = flip(away1, "x", ORDERS[1][3])
    gram = tally_call([gram] + [flip(gram, "x", s) for s in (1, 2, 3)])
    line, gram = after((line_call([own0, away0, own1, away1]), gram))
    sums = swap(line, "z")
    solver = solver_call(idx, [gram] + [flip(gram, "y", s) for s in (1, 2, 3)])
    sums, solver = after((sums, solver))
    own_sum = fold_call(sums)
    partner = other_core(own_sum)

    low_rank, share = share_call(idx, own_sum, partner, solver)

    def ortho_beside(line):
        line, late, ready = after((line, panel, solver))
        line, staged = stage_beside(line)
        return line, (staged, ortho_call(late, ready))

    mine, other, (staged, ortho) = gather_chip(low_rank, ortho_beside)
    squares = square_call(idx, mine, other)
    momentum_new = update_call(idx, staged, ortho, mine, other)
    every = squares
    for s in (1, 3, 2):
        every = every + flip(squares, "y", s)
    basis_new = share * lax.rsqrt(every[:1] / total_cols + norm_eps)
    return (momentum_new, basis_new)


def solution(mesh):
    fine = Mesh(mesh.devices.reshape(NX, NZ, NC, NY), ("x", "z", "core", "y"))
    fsdp = ("x", "z", "core")
    in_specs = (P(fsdp, "y"), P(("y", *fsdp), None))
    out_specs = (P(fsdp, "y"), P(("y", *fsdp), None))
    return jax.shard_map(
        on_device, mesh=fine, in_specs=in_specs, out_specs=out_specs, check_vma=False
    )
```

```python
import functools

import jax
import jax.numpy as jnp
from jax import lax
from jax.experimental import pallas as pl
from jax.experimental.pallas import tpu as pltpu
from jax.sharding import Mesh
from jax.sharding import PartitionSpec as P

feedback_rate = 0.05
norm_eps = 1e-06
highest = lax.Precision.HIGHEST
f32 = jnp.float32
bf16 = jnp.bfloat16

NX, NZ, NC, NY = 4, 8, 2, 4
WIDE = 128
BLOCK = 64
LINES = 5
PIECES = 2
ORDERS = ((1, 2, 0, 3), (3, 2, 0, 1))


def vmem():
    return pl.BlockSpec(memory_space=pltpu.VMEM)


def smem():
    return pl.BlockSpec(memory_space=pltpu.SMEM)


def params(mib=16):
    return pltpu.CompilerParams(vmem_limit_bytes=mib << 20)


def cost(us):
    return pl.CostEstimate(flops=int(us * 1.15e9), bytes_accessed=0, transcendentals=0)


def swap(value, axis):
    return lax.all_to_all(value, axis, 0, 0, tiled=True)


def other_core(value):
    return lax.ppermute(value, "core", [(0, 1), (1, 0)])


def flip(value, axis, bit):
    return lax.ppermute(value, axis, [(i, i ^ bit) for i in range(lax.axis_size(axis))])


def shift(value, axis, by):
    n = lax.axis_size(axis)
    return lax.ppermute(value, axis, [(i, (i + by) % n) for i in range(n)])


def gather_chip(copies, beside):
    line = swap(copies, "z")
    near, across = flip(line, "x", 1), flip(line, "x", 3)
    line, given = beside(line)
    line, given = lax.optimization_barrier((line, given))
    low, high = halves_call(near, across)
    mine = [line, near, flip(low, "x", 3), flip(high, "x", 1), across]
    return mine, [other_core(part) for part in mine], given


def pick(pieces, s, t):
    if s == 2:
        return pieces[2 + t // (NZ // 2)][t % (NZ // 2)]
    return pieces[(0, 1, None, 4)[s]][t]


def stage_kernel(momentum, out, sems):
    rows = momentum.shape[0] // sems.shape[0]
    copies = []
    for i in range(sems.shape[0]):
        at = pl.ds(i * rows, rows)
        copies.append(pltpu.make_async_copy(momentum.at[at, :], out.at[at, :], sems.at[i]))
        copies[-1].start()
    for copy in copies:
        copy.wait()


def stage_call(momentum):
    staged = pl.pallas_call(
        stage_kernel,
        in_specs=[pl.BlockSpec(memory_space=pl.ANY)],
        out_specs=vmem(),
        out_shape=pltpu.VMEM(momentum.shape, momentum.dtype),
        scratch_shapes=[pltpu.SemaphoreType.DMA((4,))],
        compiler_params=params(),
        cost_estimate=cost(2.5),
        name="stage",
    )(pltpu.with_memory_space_constraint(momentum, pltpu.HBM))
    return pltpu.with_memory_space_constraint(staged, pltpu.VMEM)


def spread_kernel(piece, out):
    for i in range(out.shape[0]):
        out[i] = piece[...]


def spread_call(piece):
    return pl.pallas_call(
        spread_kernel,
        in_specs=[vmem()],
        out_specs=vmem(),
        out_shape=jax.ShapeDtypeStruct((NZ, *piece.shape), piece.dtype),
        compiler_params=params(),
        cost_estimate=cost(0.5),
        name="spread",
    )(piece)


def halves_kernel(near, across, low, high):
    half = low.shape[0]
    low[...] = near[:half]
    high[...] = across[half:]


def halves_call(near, across):
    shape = jax.ShapeDtypeStruct((NZ // 2, *near.shape[1:]), near.dtype)
    return pl.pallas_call(
        halves_kernel,
        in_specs=[vmem()] * 2,
        out_specs=[vmem()] * 2,
        out_shape=[shape] * 2,
        compiler_params=params(),
        cost_estimate=cost(0.5),
        name="halves",
    )(near, across)


def couple_kernel(before, own, after, three, two):
    two[...] = own[...] + after[...]
    three[...] = before[...] + two[...]


def couple_call(before, own, after):
    return pl.pallas_call(
        couple_kernel,
        in_specs=[vmem()] * 3,
        out_specs=[vmem()] * 2,
        out_shape=[jax.ShapeDtypeStruct(own.shape, f32)] * 2,
        compiler_params=params(),
        cost_estimate=cost(0.6),
        name="couple",
    )(before, own, after)


def panel_kernel(idx, momentum, *refs):
    mine, other = refs[:LINES], refs[LINES : 2 * LINES]
    outs, (right, total) = refs[2 * LINES : 2 * LINES + NY], refs[2 * LINES + NY :]
    x, c, y = idx[0], idx[2], idx[3]
    half = WIDE // NC
    piece = NZ * WIDE
    for s in range(NX):
        for t in range(NZ):
            at = (x ^ s) * piece + t * WIDE
            right[pl.ds(pl.multiple_of(at + c * half, half), half), :] = pick(mine, s, t)
            right[pl.ds(pl.multiple_of(at + (1 - c) * half, half), half), :] = pick(other, s, t)
    for s in range(NX):
        at = slice(s * piece, (s + 1) * piece)
        part = jnp.dot(momentum[:, at], right[at, :], preferred_element_type=f32)
        total[...] = part if s == 0 else total[...] + part
    rows = total.shape[0] // NY
    for s in range(NY):
        outs[s][...] = total[pl.ds(pl.multiple_of((y ^ s) * rows, 8), rows), :]


def panel_call(idx, momentum, mine, other):
    rows, cols = momentum.shape
    rank = mine[0].shape[-1]
    return pl.pallas_call(
        panel_kernel,
        in_specs=[smem()] + [vmem()] * (1 + 2 * LINES),
        out_specs=[vmem()] * NY,
        out_shape=[jax.ShapeDtypeStruct((rows // NY, rank), f32)] * NY,
        scratch_shapes=[pltpu.VMEM((cols, rank), bf16), pltpu.VMEM((rows, rank), f32)],
        compiler_params=params(),
        cost_estimate=cost(3.5),
        name="panel",
    )(idx, momentum, *mine, *other)


def tally_kernel(*refs):
    refs[-1][...] = (refs[0][...] + refs[1][...]) + (refs[2][...] + refs[3][...])


def tally_call(parts):
    return pl.pallas_call(
        tally_kernel,
        in_specs=[vmem()] * len(parts),
        out_specs=vmem(),
        out_shape=jax.ShapeDtypeStruct(parts[0].shape, f32),
        compiler_params=params(),
        cost_estimate=cost(0.7),
        name="tally",
    )(*parts)


def fold_kernel(pieces, out):
    got = pieces[0]
    for i in range(1, pieces.shape[0]):
        got = got + pieces[i]
    out[...] = got


def fold_call(pieces):
    return pl.pallas_call(
        fold_kernel,
        in_specs=[vmem()],
        out_specs=vmem(),
        out_shape=jax.ShapeDtypeStruct(pieces.shape[1:], f32),
        compiler_params=params(),
        cost_estimate=cost(0.8),
        name="fold",
    )(pieces)


def prep_kernel(idx, *refs):
    parts = refs[:NY]
    panel, pieces, gram, across = refs[NY:]
    y = idx[3]
    rows = parts[0].shape[0]
    for s in range(NY):
        panel[pl.ds(pl.multiple_of((y ^ s) * rows, 8), rows), :] = parts[s][...]
    whole = panel[...]
    turned = whole.T
    rank = turned.shape[0]
    across[...] = turned
    side = rank // NY

    def product(row, count, column):
        left = across[pl.ds(pl.multiple_of(row, side // 2), count), :]
        right = across[pl.ds(pl.multiple_of(column, side), side), :]
        over = (((1,), (1,)), ((), ()))
        return lax.dot_general(left, right, over, precision=highest, preferred_element_type=f32)

    last = y == NY - 1
    below = product(jnp.where(last, y, y + 1) * side, side, jnp.where(last, 0, y) * side)
    half = product((2 + y % 2) * side + (y // 2) * (side // 2), side // 2, (y % 2) * side)
    gram[:side, :] = jnp.concatenate([product(y * side, side, y * side), below], axis=1)
    gram[side:, :] = jnp.concatenate([half[: side // 4], half[side // 4 :]], axis=1)
    for i in range(PIECES):
        now = turned.astype(bf16)
        pieces[i * rank : (i + 1) * rank, :] = now
        turned = turned - now.astype(f32)


def prep_call(idx, parts):
    rows, rank = parts[0].shape[0] * NY, parts[0].shape[1]
    return pl.pallas_call(
        prep_kernel,
        in_specs=[smem()] + [vmem()] * NY,
        out_specs=[vmem()] * 3,
        out_shape=[
            jax.ShapeDtypeStruct((rows, rank), f32),
            jax.ShapeDtypeStruct((PIECES * rank, rows), bf16),
            jax.ShapeDtypeStruct((rank // NY * 5 // 4, rank // 2), f32),
        ],
        scratch_shapes=[pltpu.VMEM((rank, rows), f32)],
        compiler_params=params(),
        cost_estimate=cost(1.5),
        name="prep",
    )(idx, *parts)


def project_kernel(part, idx, momentum, pieces, keep, send):
    x, c = idx[0], idx[2]
    rank = pieces.shape[0] // PIECES
    low = rank // 2
    first = c == 0
    wide = 2 * WIDE
    for i, s in enumerate(ORDERS[part]):
        for j in range(0, NZ // 2 * WIDE, wide):
            at = pl.multiple_of(((x ^ s) * 2 + part) * (NZ // 2 * WIDE) + j, wide)
            got = jnp.dot(pieces[...], momentum[:, pl.ds(at, wide)], preferred_element_type=f32)
            got = got[rank:] + got[:rank]
            for k in range(2):
                here = got[:, k * WIDE : (k + 1) * WIDE]
                top, bottom = here[:low], here[low:]
                keep[i, j // WIDE + k] = jnp.where(first, top, bottom)
                send[i, j // WIDE + k] = jnp.where(first, bottom, top)


def project_call(idx, momentum, pieces, part):
    rank = pieces.shape[0] // PIECES
    shape = jax.ShapeDtypeStruct((NX, NZ // 2, rank // 2, WIDE), f32)
    return pl.pallas_call(
        functools.partial(project_kernel, part),
        in_specs=[smem(), vmem(), vmem()],
        out_specs=[vmem()] * 2,
        out_shape=[shape] * 2,
        compiler_params=params(),
        cost_estimate=cost(3.5),
        name=f"project{part}",
    )(idx, momentum, pieces)


def first_kernel(keep, got, near, rest):
    for s in range(2):
        near[s] = keep[s] + got[s]
        rest[s] = keep[2 + s] + got[2 + s]


def first_call(keep, got):
    return pl.pallas_call(
        first_kernel,
        in_specs=[vmem()] * 2,
        out_specs=[vmem()] * 2,
        out_shape=[jax.ShapeDtypeStruct((2, *keep.shape[1:]), f32)] * 2,
        compiler_params=params(),
        cost_estimate=cost(0.9),
        name="first",
    )(keep, got)


def second_kernel(rest, near, own, away):
    own[...] = rest[0] + near[0]
    away[...] = rest[1] + near[1]


def second_call(rest, near):
    return pl.pallas_call(
        second_kernel,
        in_specs=[vmem()] * 2,
        out_specs=[vmem()] * 2,
        out_shape=[jax.ShapeDtypeStruct(rest.shape[1:], f32)] * 2,
        compiler_params=params(),
        cost_estimate=cost(0.9),
        name="second",
    )(rest, near)


def line_kernel(own0, near0, own1, near1, out):
    deep = own0.shape[0]
    out[:deep] = own0[...] + near0[...]
    out[deep:] = own1[...] + near1[...]


def line_call(parts):
    deep, low, wide = parts[0].shape
    return pl.pallas_call(
        line_kernel,
        in_specs=[vmem()] * len(parts),
        out_specs=vmem(),
        out_shape=jax.ShapeDtypeStruct((2 * deep, low, wide), f32),
        compiler_params=params(),
        cost_estimate=cost(0.8),
        name="line",
    )(*parts)


def share_kernel(idx, mine, other, solver, low_rank, share, turned):
    c = idx[2]
    first = c == 0
    top = jnp.where(first, mine[...], other[...])
    bottom = jnp.where(first, other[...], mine[...])
    whole = jnp.concatenate([top, bottom], axis=0)
    got = jnp.dot(solver[...], whole, precision=highest, preferred_element_type=f32)
    low = got.shape[0] // 2
    rounded = jnp.where(first, got[:low], got[low:]).astype(bf16)
    for t in range(NZ):
        low_rank[t] = rounded
    turned[...] = got.T
    half = WIDE // NC
    share[...] = turned[pl.ds(pl.multiple_of(c * half, half), half), :]


def share_call(idx, mine, other, solver):
    low, wide = mine.shape
    rank = 2 * low
    return pl.pallas_call(
        share_kernel,
        in_specs=[smem()] + [vmem()] * 3,
        out_specs=[vmem()] * 2,
        out_shape=[
            jax.ShapeDtypeStruct((NZ, low, wide), bf16),
            jax.ShapeDtypeStruct((wide // NC, rank), f32),
        ],
        scratch_shapes=[pltpu.VMEM((wide, rank), f32)],
        compiler_params=params(),
        cost_estimate=cost(1.0),
        name="share",
    )(idx, mine, other, solver)


def ortho_kernel(panel, solver, ortho):
    across = (((1,), (1,)), ((), ()))
    ortho[...] = lax.dot_general(
        panel[...], solver[...], across, precision=highest, preferred_element_type=f32
    ).astype(bf16)


def ortho_call(panel, solver):
    rows, rank = panel.shape
    return pl.pallas_call(
        ortho_kernel,
        in_specs=[vmem()] * 2,
        out_specs=vmem(),
        out_shape=jax.ShapeDtypeStruct((rows, rank), bf16),
        compiler_params=params(),
        cost_estimate=cost(0.7),
        name="ortho",
    )(panel, solver)


def square_kernel(idx, *refs):
    mine, other, out = refs[:LINES], refs[LINES : 2 * LINES], refs[-1]
    c = idx[2]

    def total(group):
        acc = None
        for ref in group:
            for t in range(ref.shape[0]):
                v = ref[t].astype(f32)
                acc = v * v if acc is None else acc + v * v
        return jnp.sum(acc, axis=1, keepdims=True)

    a, b = total(mine), total(other)
    first = c == 0
    whole = jnp.concatenate([jnp.where(first, a, b), jnp.where(first, b, a)], axis=0)
    out[...] = jnp.broadcast_to(whole, (whole.shape[0], WIDE)).T[:8]


def square_call(idx, mine, other):
    low = mine[0].shape[1]
    return pl.pallas_call(
        square_kernel,
        in_specs=[smem()] + [vmem()] * (2 * LINES),
        out_specs=vmem(),
        out_shape=jax.ShapeDtypeStruct((8, 2 * low), f32),
        compiler_params=params(),
        cost_estimate=cost(1.0),
        name="square",
    )(idx, *mine, *other)


def update_kernel(idx, momentum, ortho, *refs):
    mine, other = refs[:LINES], refs[LINES : 2 * LINES]
    out, fresh, right, sems = refs[2 * LINES :]
    x, c = idx[0], idx[2]
    piece = NZ * WIDE
    low = right.shape[0] // 2
    for s in range(NX):
        for t in range(NZ):
            at = pl.ds(pl.multiple_of((x ^ s) * piece + t * WIDE, WIDE), WIDE)
            right[pl.ds(pl.multiple_of(c * low, low), low), at] = pick(mine, s, t)
            right[pl.ds(pl.multiple_of((1 - c) * low, low), low), at] = pick(other, s, t)
    outward = []
    for s in range(NX):
        for j in range(s * piece, (s + 1) * piece, 2 * WIDE):
            at = slice(j, j + 2 * WIDE)
            got = jnp.dot(ortho[...], right[:, at], preferred_element_type=f32)
            fresh[:, at] = (momentum[:, at].astype(f32) - feedback_rate * got).astype(bf16)
        at = pl.ds(s * piece, piece)
        outward.append(pltpu.make_async_copy(fresh.at[:, at], out.at[:, at], sems.at[s]))
        outward[-1].start()
    for copy in outward:
        copy.wait()


def update_call(idx, momentum, ortho, mine, other):
    rows, cols = momentum.shape
    rank = ortho.shape[1]
    return pl.pallas_call(
        update_kernel,
        in_specs=[smem()] + [vmem()] * (2 + 2 * LINES),
        out_specs=pl.BlockSpec(memory_space=pl.ANY),
        out_shape=jax.ShapeDtypeStruct((rows, cols), bf16),
        scratch_shapes=[
            pltpu.VMEM((rows, cols), bf16),
            pltpu.VMEM((rank, cols), bf16),
            pltpu.SemaphoreType.DMA((NX,)),
        ],
        compiler_params=params(),
        cost_estimate=cost(5.0),
        name="update",
    )(idx, momentum, ortho, *mine, *other)


def invert_block(block):
    size = block.shape[0]
    strips = size // 8
    row = lax.broadcasted_iota(jnp.int32, (8, 2 * size), 0)
    eye = (
        lax.broadcasted_iota(jnp.int32, (size, size), 0)
        == lax.broadcasted_iota(jnp.int32, (size, size), 1)
    ).astype(f32)
    both = jnp.concatenate([eye, block], axis=1)
    wide = [both[8 * t : 8 * t + 8] for t in range(strips)]
    shape = (8, 2 * size)
    done = []
    for s in range(strips):
        cols = {
            t: [jnp.broadcast_to(wide[t][:, size + 8 * s + j : size + 8 * s + j + 1], shape) for j in range(8)]
            for t in range(s, strips)
        }
        scale = jnp.ones(shape, f32)
        for k in range(8):
            over = lambda v: jnp.broadcast_to(v[k : k + 1], shape)
            pivot = over(cols[s][k])
            inverse = 1.0 / pivot
            scale = jnp.where(row == k, lax.rsqrt(pivot), scale)
            lead = over(wide[s])
            heads = {j: over(cols[s][j]) for j in range(k + 1, 8)}
            for t in range(s, strips):
                factor = cols[t][k] * inverse
                if t == s:
                    factor = jnp.where(row > k, factor, 0.0)
                wide[t] = wide[t] - factor * lead
                for j in range(k + 1, 8):
                    cols[t][j] = cols[t][j] - factor * heads[j]
        done.append(wide[s] * scale)
    return jnp.concatenate(done, axis=0)[:, :size]

def solver_kernel(idx, *refs):
    parts, (out, left, right, held) = refs[:NY], refs[NY:]
    rank = out.shape[0]
    side = rank // NY
    for s in range(NY):
        held[idx[3] ^ s] = parts[s][...]
    left[...] = jnp.zeros_like(left)
    for y in range(NY):
        here = slice(y * side, (y + 1) * side)
        left[here, here] = held[y, :side, :side]
        if y == NY - 1:
            left[here, :side] = held[y, :side, side:]
        else:
            left[(y + 1) * side : (y + 2) * side, here] = held[y, :side, side:]
        row, column = (2 + y % 2) * side + y // 2 * (side // 2), (y % 2) * side
        for i in range(2):
            at = row + i * (side // 4)
            left[at : at + side // 4, column : column + side] = held[y, side:, i * side : (i + 1) * side]
    right[...] = (
        lax.broadcasted_iota(jnp.int32, (rank, rank), 0)
        == lax.broadcasted_iota(jnp.int32, (rank, rank), 1)
    ).astype(f32)
    across = (((1,), (1,)), ((), ()))
    for at in range(0, rank, BLOCK):
        end = at + BLOCK
        inverse = invert_block(left[at:end, at:end])
        rows = jnp.dot(inverse, right[at:end, :end], precision=highest, preferred_element_type=f32)
        out[at:end, :end] = rows
        if end < rank:
            out[at:end, end:] = jnp.zeros((BLOCK, rank - end), f32)
            down = lax.dot_general(left[end:, at:end], inverse, across, precision=highest, preferred_element_type=f32)
            left[end:, end:] -= lax.dot_general(down, down, across, precision=highest, preferred_element_type=f32)
            right[end:, :end] -= jnp.dot(down, rows, precision=highest, preferred_element_type=f32)

def solver_call(idx, parts):
    rank = 2 * parts[0].shape[1]
    return pl.pallas_call(
        solver_kernel,
        in_specs=[smem()] + [vmem()] * NY,
        out_specs=vmem(),
        out_shape=jax.ShapeDtypeStruct((rank, rank), f32),
        scratch_shapes=[pltpu.VMEM((rank, rank), f32)] * 2 + [pltpu.VMEM((NY, *parts[0].shape), f32)],
        compiler_params=params(),
        cost_estimate=cost(9.4),
        name="solver",
    )(idx, *parts)


def on_device(momentum, basis):
    total_cols = momentum.shape[1] * NY
    rank = basis.shape[1]
    x, z, c, y = (lax.axis_index(axis) for axis in ("x", "z", "core", "y"))
    idx = jnp.stack([x, z, c, y] + [x ^ s for order in ORDERS for s in order]).astype(jnp.int32)

    after = lax.optimization_barrier

    def stage_beside(line):
        line, late, _ = after((line, momentum, idx))
        return line, stage_call(late)

    mine, other, staged = gather_chip(spread_call(basis), stage_beside)
    parts = panel_call(idx, staged, mine, other)
    own = tally_call([parts[0]] + [flip(parts[s], "y", s) for s in (1, 3, 2)])
    panel, pieces, gram = prep_call(idx, [own] + [flip(own, "y", s) for s in (1, 2, 3)])

    keep0, send0 = project_call(idx, staged, pieces, 0)
    got0 = other_core(send0)
    gram = gram + other_core(gram)
    gram = tally_call([gram] + [flip(gram, "x", s) for s in (1, 2, 3)])
    pieces, gram = after((pieces, gram))
    keep1, send1 = project_call(idx, staged, pieces, 1)
    got1 = other_core(send1)
    near0, rest0 = first_call(keep0, got0)
    near0 = flip(near0, "x", ORDERS[0][0])
    near1, rest1 = first_call(keep1, got1)
    near1, gram = after((near1, gram))
    near1 = flip(near1, "x", ORDERS[1][0])
    three, two = couple_call(shift(gram, "z", 1), gram, shift(gram, "z", -1))
    rest0, three, two = after((rest0, three, two))
    gram = (three + shift(two, "z", 3)) + shift(three, "z", -3)
    own0, away0 = second_call(rest0, near0)
    away0 = flip(away0, "x", ORDERS[0][3])
    rest1, gram = after((rest1, gram))
    own1, away1 = second_call(rest1, near1)
    away1 = flip(away1, "x", ORDERS[1][3])
    quarters = [gram] + [flip(gram, "y", s) for s in (1, 2, 3)]
    line, quarters = after((line_call([own0, away0, own1, away1]), quarters))
    sums = swap(line, "z")
    solver = solver_call(idx, quarters)
    sums, solver = after((sums, solver))
    own_sum = fold_call(sums)
    partner = other_core(own_sum)

    low_rank, share = share_call(idx, own_sum, partner, solver)

    def ortho_beside(line):
        line, late, ready = after((line, panel, solver))
        line, staged = stage_beside(line)
        return line, (staged, ortho_call(late, ready))

    mine, other, (staged, ortho) = gather_chip(low_rank, ortho_beside)
    squares = square_call(idx, mine, other)
    momentum_new = update_call(idx, staged, ortho, mine, other)
    every = squares
    for s in (1, 3, 2):
        every = every + flip(squares, "y", s)
    basis_new = share * lax.rsqrt(every[:1] / total_cols + norm_eps)
    return (momentum_new, basis_new)


def solution(mesh):
    fine = Mesh(mesh.devices.reshape(NX, NZ, NC, NY), ("x", "z", "core", "y"))
    fsdp = ("x", "z", "core")
    in_specs = (P(fsdp, "y"), P(("y", *fsdp), None))
    out_specs = (P(fsdp, "y"), P(("y", *fsdp), None))
    return jax.shard_map(
        on_device, mesh=fine, in_specs=in_specs, out_specs=out_specs, check_vma=False
    )
```

```python
import functools

import jax
import jax.numpy as jnp
from jax import lax
from jax.experimental import pallas as pl
from jax.experimental.pallas import tpu as pltpu
from jax.sharding import Mesh
from jax.sharding import PartitionSpec as P

feedback_rate = 0.05
norm_eps = 1e-06
highest = lax.Precision.HIGHEST
f32 = jnp.float32
bf16 = jnp.bfloat16

NX, NZ, NC, NY = 4, 8, 2, 4
WIDE = 128
BLOCK = 64
PIECES = 2
ORDERS = ((1, 2, 0, 3), (3, 2, 0, 1))


def vmem():
    return pl.BlockSpec(memory_space=pltpu.VMEM)


def smem():
    return pl.BlockSpec(memory_space=pltpu.SMEM)


def params(mib=16):
    return pltpu.CompilerParams(vmem_limit_bytes=mib << 20)


def cost(us):
    return pl.CostEstimate(flops=int(us * 1.15e9), bytes_accessed=0, transcendentals=0)


def swap(value, axis):
    return lax.all_to_all(value, axis, 0, 0, tiled=True)


def other_core(value):
    return lax.ppermute(value, "core", [(0, 1), (1, 0)])


def flip(value, axis, bit):
    return lax.ppermute(value, axis, [(i, i ^ bit) for i in range(lax.axis_size(axis))])


def gather_chip(copies, beside):
    line = swap(copies, "z")
    near, across, far = flip(line, "x", 1), flip(line, "x", 3), flip(line, "x", 2)
    line, given = beside(line)
    line, given = lax.optimization_barrier((line, given))
    mine = [line, near, far, across]
    return mine, [other_core(part) for part in mine], given


def stage_kernel(momentum, out, sems):
    rows = momentum.shape[0] // sems.shape[0]
    copies = []
    for i in range(sems.shape[0]):
        at = pl.ds(i * rows, rows)
        copies.append(pltpu.make_async_copy(momentum.at[at, :], out.at[at, :], sems.at[i]))
        copies[-1].start()
    for copy in copies:
        copy.wait()


def stage_call(momentum):
    staged = pl.pallas_call(
        stage_kernel,
        in_specs=[pl.BlockSpec(memory_space=pl.ANY)],
        out_specs=vmem(),
        out_shape=pltpu.VMEM(momentum.shape, momentum.dtype),
        scratch_shapes=[pltpu.SemaphoreType.DMA((4,))],
        compiler_params=params(),
        cost_estimate=cost(2.5),
        name="stage",
    )(pltpu.with_memory_space_constraint(momentum, pltpu.HBM))
    return pltpu.with_memory_space_constraint(staged, pltpu.VMEM)


def spread_kernel(piece, out, sems):
    copies = [pltpu.make_async_copy(piece, out.at[i], sems.at[i]) for i in range(out.shape[0])]
    for copy in copies:
        copy.start()
    for copy in copies:
        copy.wait()


def spread_call(piece):
    return pl.pallas_call(
        spread_kernel,
        in_specs=[pl.BlockSpec(memory_space=pl.ANY)],
        out_specs=vmem(),
        out_shape=jax.ShapeDtypeStruct((NZ, *piece.shape), piece.dtype),
        scratch_shapes=[pltpu.SemaphoreType.DMA((NZ,))],
        compiler_params=params(),
        cost_estimate=cost(0.7),
        name="spread",
    )(pltpu.with_memory_space_constraint(piece, pltpu.HBM))


def panel_kernel(idx, momentum, *refs):
    mine, other = refs[:NX], refs[NX : 2 * NX]
    outs, (right, total) = refs[2 * NX : 2 * NX + NY], refs[2 * NX + NY :]
    x, c, y = idx[0], idx[2], idx[3]
    half = WIDE // NC
    piece = NZ * WIDE
    for s in range(NX):
        for t in range(NZ):
            at = (x ^ s) * piece + t * WIDE
            right[pl.ds(pl.multiple_of(at + c * half, half), half), :] = mine[s][t]
            right[pl.ds(pl.multiple_of(at + (1 - c) * half, half), half), :] = other[s][t]
    for s in range(NX):
        at = slice(s * piece, (s + 1) * piece)
        part = jnp.dot(momentum[:, at], right[at, :], preferred_element_type=f32)
        total[...] = part if s == 0 else total[...] + part
    rows = total.shape[0] // NY
    for s in range(NY):
        outs[s][...] = total[pl.ds(pl.multiple_of((y ^ s) * rows, 8), rows), :]


def panel_call(idx, momentum, mine, other):
    rows, cols = momentum.shape
    rank = mine[0].shape[-1]
    return pl.pallas_call(
        panel_kernel,
        in_specs=[smem()] + [vmem()] * (1 + 2 * NX),
        out_specs=[vmem()] * NY,
        out_shape=[jax.ShapeDtypeStruct((rows // NY, rank), f32)] * NY,
        scratch_shapes=[pltpu.VMEM((cols, rank), bf16), pltpu.VMEM((rows, rank), f32)],
        compiler_params=params(),
        cost_estimate=cost(3.5),
        name="panel",
    )(idx, momentum, *mine, *other)


def tally_kernel(*refs):
    refs[-1][...] = (refs[0][...] + refs[1][...]) + (refs[2][...] + refs[3][...])


def tally_call(parts):
    return pl.pallas_call(
        tally_kernel,
        in_specs=[vmem()] * len(parts),
        out_specs=vmem(),
        out_shape=jax.ShapeDtypeStruct(parts[0].shape, f32),
        compiler_params=params(),
        cost_estimate=cost(0.7),
        name="tally",
    )(*parts)


def fold_kernel(pieces, out):
    got = pieces[0]
    for i in range(1, pieces.shape[0]):
        got = got + pieces[i]
    out[...] = got


def fold_call(pieces):
    return pl.pallas_call(
        fold_kernel,
        in_specs=[vmem()],
        out_specs=vmem(),
        out_shape=jax.ShapeDtypeStruct(pieces.shape[1:], f32),
        compiler_params=params(),
        cost_estimate=cost(0.8),
        name="fold",
    )(pieces)


def prep_kernel(idx, *refs):
    parts = refs[:NY]
    panel, pieces, gram, across = refs[NY:]
    y = idx[3]
    rows = parts[0].shape[0]
    for s in range(NY):
        panel[pl.ds(pl.multiple_of((y ^ s) * rows, 8), rows), :] = parts[s][...]
    whole = panel[...]
    turned = whole.T
    rank = turned.shape[0]
    across[...] = turned
    side = rank // NY

    def product(row, count, column):
        left = across[pl.ds(pl.multiple_of(row, side // 2), count), :]
        right = across[pl.ds(pl.multiple_of(column, side), side), :]
        over = (((1,), (1,)), ((), ()))
        return lax.dot_general(left, right, over, precision=highest, preferred_element_type=f32)

    last = y == NY - 1
    below = product(jnp.where(last, y, y + 1) * side, side, jnp.where(last, 0, y) * side)
    half = product((2 + y % 2) * side + (y // 2) * (side // 2), side // 2, (y % 2) * side)
    gram[:side, :] = jnp.concatenate([product(y * side, side, y * side), below], axis=1)
    gram[side:, :] = jnp.concatenate([half[: side // 4], half[side // 4 :]], axis=1)
    for i in range(PIECES):
        now = turned.astype(bf16)
        pieces[i * rank : (i + 1) * rank, :] = now
        turned = turned - now.astype(f32)


def prep_call(idx, parts):
    rows, rank = parts[0].shape[0] * NY, parts[0].shape[1]
    return pl.pallas_call(
        prep_kernel,
        in_specs=[smem()] + [vmem()] * NY,
        out_specs=[vmem()] * 3,
        out_shape=[
            jax.ShapeDtypeStruct((rows, rank), f32),
            jax.ShapeDtypeStruct((PIECES * rank, rows), bf16),
            jax.ShapeDtypeStruct((rank // NY * 5 // 4, rank // 2), f32),
        ],
        scratch_shapes=[pltpu.VMEM((rank, rows), f32)],
        compiler_params=params(),
        cost_estimate=cost(1.5),
        name="prep",
    )(idx, *parts)


def project_kernel(part, idx, momentum, pieces, keep, send):
    x, c = idx[0], idx[2]
    rank = pieces.shape[0] // PIECES
    low = rank // 2
    first = c == 0
    wide = 2 * WIDE
    for i, s in enumerate(ORDERS[part]):
        for j in range(0, NZ // 2 * WIDE, wide):
            at = pl.multiple_of(((x ^ s) * 2 + part) * (NZ // 2 * WIDE) + j, wide)
            got = jnp.dot(pieces[...], momentum[:, pl.ds(at, wide)], preferred_element_type=f32)
            got = got[rank:] + got[:rank]
            for k in range(2):
                here = got[:, k * WIDE : (k + 1) * WIDE]
                top, bottom = here[:low], here[low:]
                keep[i, j // WIDE + k] = jnp.where(first, top, bottom)
                send[i, j // WIDE + k] = jnp.where(first, bottom, top)


def project_call(idx, momentum, pieces, part):
    rank = pieces.shape[0] // PIECES
    shape = jax.ShapeDtypeStruct((NX, NZ // 2, rank // 2, WIDE), f32)
    return pl.pallas_call(
        functools.partial(project_kernel, part),
        in_specs=[smem(), vmem(), vmem()],
        out_specs=[vmem()] * 2,
        out_shape=[shape] * 2,
        compiler_params=params(),
        cost_estimate=cost(3.5),
        name=f"project{part}",
    )(idx, momentum, pieces)


def first_kernel(keep, got, near, rest):
    for s in range(2):
        near[s] = keep[s] + got[s]
        rest[s] = keep[2 + s] + got[2 + s]


def first_call(keep, got):
    return pl.pallas_call(
        first_kernel,
        in_specs=[vmem()] * 2,
        out_specs=[vmem()] * 2,
        out_shape=[jax.ShapeDtypeStruct((2, *keep.shape[1:]), f32)] * 2,
        compiler_params=params(),
        cost_estimate=cost(0.9),
        name="first",
    )(keep, got)


def second_kernel(rest, near, own, away):
    own[...] = rest[0] + near[0]
    away[...] = rest[1] + near[1]


def second_call(rest, near):
    return pl.pallas_call(
        second_kernel,
        in_specs=[vmem()] * 2,
        out_specs=[vmem()] * 2,
        out_shape=[jax.ShapeDtypeStruct(rest.shape[1:], f32)] * 2,
        compiler_params=params(),
        cost_estimate=cost(0.9),
        name="second",
    )(rest, near)


def line_kernel(own0, near0, own1, near1, out):
    deep = own0.shape[0]
    out[:deep] = own0[...] + near0[...]
    out[deep:] = own1[...] + near1[...]


def line_call(parts):
    deep, low, wide = parts[0].shape
    return pl.pallas_call(
        line_kernel,
        in_specs=[vmem()] * len(parts),
        out_specs=vmem(),
        out_shape=jax.ShapeDtypeStruct((2 * deep, low, wide), f32),
        compiler_params=params(),
        cost_estimate=cost(0.8),
        name="line",
    )(*parts)


def share_kernel(idx, mine, other, solver, low_rank, share, turned):
    c = idx[2]
    first = c == 0
    top = jnp.where(first, mine[...], other[...])
    bottom = jnp.where(first, other[...], mine[...])
    whole = jnp.concatenate([top, bottom], axis=0)
    got = jnp.dot(solver[...], whole, precision=highest, preferred_element_type=f32)
    low = got.shape[0] // 2
    rounded = jnp.where(first, got[:low], got[low:]).astype(bf16)
    for t in range(NZ):
        low_rank[t] = rounded
    turned[...] = got.T
    half = WIDE // NC
    share[...] = turned[pl.ds(pl.multiple_of(c * half, half), half), :]


def share_call(idx, mine, other, solver):
    low, wide = mine.shape
    rank = 2 * low
    return pl.pallas_call(
        share_kernel,
        in_specs=[smem()] + [vmem()] * 3,
        out_specs=[vmem()] * 2,
        out_shape=[
            jax.ShapeDtypeStruct((NZ, low, wide), bf16),
            jax.ShapeDtypeStruct((wide // NC, rank), f32),
        ],
        scratch_shapes=[pltpu.VMEM((wide, rank), f32)],
        compiler_params=params(),
        cost_estimate=cost(1.0),
        name="share",
    )(idx, mine, other, solver)


def ortho_kernel(panel, solver, ortho):
    across = (((1,), (1,)), ((), ()))
    ortho[...] = lax.dot_general(
        panel[...], solver[...], across, precision=highest, preferred_element_type=f32
    ).astype(bf16)


def ortho_call(panel, solver):
    rows, rank = panel.shape
    return pl.pallas_call(
        ortho_kernel,
        in_specs=[vmem()] * 2,
        out_specs=vmem(),
        out_shape=jax.ShapeDtypeStruct((rows, rank), bf16),
        compiler_params=params(),
        cost_estimate=cost(0.7),
        name="ortho",
    )(panel, solver)


def square_kernel(idx, *refs):
    mine, other, out = refs[:NX], refs[NX : 2 * NX], refs[-1]
    c = idx[2]

    def total(group):
        acc = None
        for ref in group:
            for t in range(NZ):
                v = ref[t].astype(f32)
                acc = v * v if acc is None else acc + v * v
        return jnp.sum(acc, axis=1, keepdims=True)

    a, b = total(mine), total(other)
    first = c == 0
    whole = jnp.concatenate([jnp.where(first, a, b), jnp.where(first, b, a)], axis=0)
    out[...] = jnp.broadcast_to(whole, (whole.shape[0], WIDE)).T[:8]


def square_call(idx, mine, other):
    low = mine[0].shape[1]
    return pl.pallas_call(
        square_kernel,
        in_specs=[smem()] + [vmem()] * (2 * NX),
        out_specs=vmem(),
        out_shape=jax.ShapeDtypeStruct((8, 2 * low), f32),
        compiler_params=params(),
        cost_estimate=cost(1.0),
        name="square",
    )(idx, *mine, *other)


def update_kernel(idx, momentum, ortho, *refs):
    mine, other = refs[:NX], refs[NX : 2 * NX]
    out, fresh, right, sems = refs[2 * NX :]
    x, c = idx[0], idx[2]
    piece = NZ * WIDE
    low = right.shape[0] // 2
    for s in range(NX):
        for t in range(NZ):
            at = pl.ds(pl.multiple_of((x ^ s) * piece + t * WIDE, WIDE), WIDE)
            right[pl.ds(pl.multiple_of(c * low, low), low), at] = mine[s][t]
            right[pl.ds(pl.multiple_of((1 - c) * low, low), low), at] = other[s][t]
    outward = []
    for s in range(NX):
        for j in range(s * piece, (s + 1) * piece, 2 * WIDE):
            at = slice(j, j + 2 * WIDE)
            got = jnp.dot(ortho[...], right[:, at], preferred_element_type=f32)
            fresh[:, at] = (momentum[:, at].astype(f32) - feedback_rate * got).astype(bf16)
        at = pl.ds(s * piece, piece)
        outward.append(pltpu.make_async_copy(fresh.at[:, at], out.at[:, at], sems.at[s]))
        outward[-1].start()
    for copy in outward:
        copy.wait()


def update_call(idx, momentum, ortho, mine, other):
    rows, cols = momentum.shape
    rank = ortho.shape[1]
    return pl.pallas_call(
        update_kernel,
        in_specs=[smem()] + [vmem()] * (2 + 2 * NX),
        out_specs=pl.BlockSpec(memory_space=pl.ANY),
        out_shape=jax.ShapeDtypeStruct((rows, cols), bf16),
        scratch_shapes=[
            pltpu.VMEM((rows, cols), bf16),
            pltpu.VMEM((rank, cols), bf16),
            pltpu.SemaphoreType.DMA((NX,)),
        ],
        compiler_params=params(),
        cost_estimate=cost(5.0),
        name="update",
    )(idx, momentum, ortho, *mine, *other)


def invert_block(block):
    size = block.shape[0]
    strips = size // 8
    row = lax.broadcasted_iota(jnp.int32, (8, 2 * size), 0)
    eye = (
        lax.broadcasted_iota(jnp.int32, (size, size), 0)
        == lax.broadcasted_iota(jnp.int32, (size, size), 1)
    ).astype(f32)
    both = jnp.concatenate([eye, block], axis=1)
    wide = [both[8 * t : 8 * t + 8] for t in range(strips)]
    shape = (8, 2 * size)
    done = []
    for s in range(strips):
        cols = {
            t: [jnp.broadcast_to(wide[t][:, size + 8 * s + j : size + 8 * s + j + 1], shape) for j in range(8)]
            for t in range(s, strips)
        }
        scale = jnp.ones(shape, f32)
        for k in range(8):
            over = lambda v: jnp.broadcast_to(v[k : k + 1], shape)
            pivot = over(cols[s][k])
            inverse = 1.0 / pivot
            scale = jnp.where(row == k, lax.rsqrt(pivot), scale)
            lead = over(wide[s])
            heads = {j: over(cols[s][j]) for j in range(k + 1, 8)}
            for t in range(s, strips):
                factor = cols[t][k] * inverse
                if t == s:
                    factor = jnp.where(row > k, factor, 0.0)
                wide[t] = wide[t] - factor * lead
                for j in range(k + 1, 8):
                    cols[t][j] = cols[t][j] - factor * heads[j]
        done.append(wide[s] * scale)
    return jnp.concatenate(done, axis=0)[:, :size]

def solver_kernel(idx, *refs):
    parts, (out, left, right, held) = refs[:NY], refs[NY:]
    rank = out.shape[0]
    side = rank // NY
    for s in range(NY):
        held[idx[3] ^ s] = parts[s][...]
    left[...] = jnp.zeros_like(left)
    for y in range(NY):
        here = slice(y * side, (y + 1) * side)
        left[here, here] = held[y, :side, :side]
        if y == NY - 1:
            left[here, :side] = held[y, :side, side:]
        else:
            left[(y + 1) * side : (y + 2) * side, here] = held[y, :side, side:]
        row, column = (2 + y % 2) * side + y // 2 * (side // 2), (y % 2) * side
        for i in range(2):
            at = row + i * (side // 4)
            left[at : at + side // 4, column : column + side] = held[y, side:, i * side : (i + 1) * side]
    right[...] = (
        lax.broadcasted_iota(jnp.int32, (rank, rank), 0)
        == lax.broadcasted_iota(jnp.int32, (rank, rank), 1)
    ).astype(f32)
    across = (((1,), (1,)), ((), ()))
    for at in range(0, rank, BLOCK):
        end = at + BLOCK
        inverse = invert_block(left[at:end, at:end])
        rows = jnp.dot(inverse, right[at:end, :end], precision=highest, preferred_element_type=f32)
        out[at:end, :end] = rows
        if end < rank:
            out[at:end, end:] = jnp.zeros((BLOCK, rank - end), f32)
            down = lax.dot_general(left[end:, at:end], inverse, across, precision=highest, preferred_element_type=f32)
            left[end:, end:] -= lax.dot_general(down, down, across, precision=highest, preferred_element_type=f32)
            right[end:, :end] -= jnp.dot(down, rows, precision=highest, preferred_element_type=f32)

def solver_call(idx, parts):
    rank = 2 * parts[0].shape[1]
    return pl.pallas_call(
        solver_kernel,
        in_specs=[smem()] + [vmem()] * NY,
        out_specs=vmem(),
        out_shape=jax.ShapeDtypeStruct((rank, rank), f32),
        scratch_shapes=[pltpu.VMEM((rank, rank), f32)] * 2 + [pltpu.VMEM((NY, *parts[0].shape), f32)],
        compiler_params=params(),
        cost_estimate=cost(9.4),
        name="solver",
    )(idx, *parts)


def on_device(momentum, basis):
    total_cols = momentum.shape[1] * NY
    rank = basis.shape[1]
    x, z, c, y = (lax.axis_index(axis) for axis in ("x", "z", "core", "y"))
    idx = jnp.stack([x, z, c, y] + [x ^ s for order in ORDERS for s in order]).astype(jnp.int32)

    after = lax.optimization_barrier

    def stage_beside(line):
        line, late, _ = after((line, momentum, idx))
        return line, stage_call(late)

    mine, other, staged = gather_chip(spread_call(basis), stage_beside)
    parts = panel_call(idx, staged, mine, other)
    own = tally_call([parts[0]] + [flip(parts[s], "y", s) for s in (1, 3, 2)])
    panel, pieces, gram = prep_call(idx, [own] + [flip(own, "y", s) for s in (1, 2, 3)])

    keep0, send0 = project_call(idx, staged, pieces, 0)
    got0 = other_core(send0)
    gram = gram + other_core(gram)
    gram = tally_call([gram] + [flip(gram, "x", s) for s in (1, 2, 3)])
    pieces, gram = after((pieces, gram))
    keep1, send1 = project_call(idx, staged, pieces, 1)
    got1 = other_core(send1)
    near0, rest0 = first_call(keep0, got0)
    near0 = flip(near0, "x", ORDERS[0][0])
    near1, rest1 = first_call(keep1, got1)
    near1, gram = after((near1, gram))
    near1 = flip(near1, "x", ORDERS[1][0])
    gram = tally_call([gram] + [flip(gram, "z", s) for s in (1, 2, 3)])
    rest0, gram = after((rest0, gram))
    opposite = flip(gram, "z", 4)
    own0, away0 = second_call(rest0, near0)
    away0 = flip(away0, "x", ORDERS[0][3])
    rest1, opposite = after((rest1, opposite))
    own1, away1 = second_call(rest1, near1)
    away1 = flip(away1, "x", ORDERS[1][3])
    gram = gram + opposite
    quarters = [gram] + [flip(gram, "y", s) for s in (1, 2, 3)]
    line, quarters = after((line_call([own0, away0, own1, away1]), quarters))
    sums = swap(line, "z")
    solver = solver_call(idx, quarters)
    sums, solver = after((sums, solver))
    own_sum = fold_call(sums)
    partner = other_core(own_sum)

    low_rank, share = share_call(idx, own_sum, partner, solver)

    def ortho_beside(line):
        line, staged = stage_beside(line)
        staged, late = after((staged, panel))
        return line, (staged, ortho_call(late, solver))

    mine, other, (staged, ortho) = gather_chip(low_rank, ortho_beside)
    squares = square_call(idx, mine, other)
    momentum_new = update_call(idx, staged, ortho, mine, other)
    every = squares
    for s in (1, 3, 2):
        every = every + flip(squares, "y", s)
    basis_new = share * lax.rsqrt(every[:1] / total_cols + norm_eps)
    return (momentum_new, basis_new)


def solution(mesh):
    fine = Mesh(mesh.devices.reshape(NX, NZ, NC, NY), ("x", "z", "core", "y"))
    fsdp = ("x", "z", "core")
    in_specs = (P(fsdp, "y"), P(("y", *fsdp), None))
    out_specs = (P(fsdp, "y"), P(("y", *fsdp), None))
    return jax.shard_map(
        on_device, mesh=fine, in_specs=in_specs, out_specs=out_specs, check_vma=False
    )
```

```python
import functools

import jax
import jax.numpy as jnp
from jax import lax
from jax.experimental import pallas as pl
from jax.experimental.pallas import tpu as pltpu
from jax.sharding import Mesh
from jax.sharding import PartitionSpec as P

feedback_rate = 0.05
norm_eps = 1e-06
highest = lax.Precision.HIGHEST
f32 = jnp.float32
bf16 = jnp.bfloat16

NX, NZ, NC, NY = 4, 8, 2, 4
WIDE = 128
BLOCK = 64
PARTNERS = (0, 1, 3, 2)
PIECES = 2
ORDERS = ((1, 2, 0, 3), (3, 2, 0, 1))


def vmem():
    return pl.BlockSpec(memory_space=pltpu.VMEM)


def smem():
    return pl.BlockSpec(memory_space=pltpu.SMEM)


def params(mib=16):
    return pltpu.CompilerParams(vmem_limit_bytes=mib << 20)


def cost(us):
    return pl.CostEstimate(flops=int(us * 1.15e9), bytes_accessed=0, transcendentals=0)


def swap(value, axis):
    return lax.all_to_all(value, axis, 0, 0, tiled=True)


def other_core(value):
    return lax.ppermute(value, "core", [(0, 1), (1, 0)])


def flip(value, axis, bit):
    return lax.ppermute(value, axis, [(i, i ^ bit) for i in range(lax.axis_size(axis))])


def gather_chip(copies, beside):
    line = swap(copies, "z")
    near, across, far = flip(line, "x", 1), flip(line, "x", 3), flip(line, "x", 2)
    line, given = beside(line)
    line, given = lax.optimization_barrier((line, given))
    mine = [line, near, far, across]
    return mine, [other_core(part) for part in mine], given


def stage_kernel(momentum, out, sems):
    rows = momentum.shape[0] // sems.shape[0]
    copies = []
    for i in range(sems.shape[0]):
        at = pl.ds(i * rows, rows)
        copies.append(pltpu.make_async_copy(momentum.at[at, :], out.at[at, :], sems.at[i]))
        copies[-1].start()
    for copy in copies:
        copy.wait()


def stage_call(momentum):
    staged = pl.pallas_call(
        stage_kernel,
        in_specs=[pl.BlockSpec(memory_space=pl.ANY)],
        out_specs=vmem(),
        out_shape=pltpu.VMEM(momentum.shape, momentum.dtype),
        scratch_shapes=[pltpu.SemaphoreType.DMA((4,))],
        compiler_params=params(),
        cost_estimate=cost(2.5),
        name="stage",
    )(pltpu.with_memory_space_constraint(momentum, pltpu.HBM))
    return pltpu.with_memory_space_constraint(staged, pltpu.VMEM)


def spread_kernel(piece, out):
    for i in range(out.shape[0]):
        out[i] = piece[...]


def spread_call(piece):
    return pl.pallas_call(
        spread_kernel,
        in_specs=[vmem()],
        out_specs=vmem(),
        out_shape=jax.ShapeDtypeStruct((NZ, *piece.shape), piece.dtype),
        compiler_params=params(),
        cost_estimate=cost(0.5),
        name="spread",
    )(piece)


def panel_kernel(idx, momentum, *refs):
    mine, other = refs[:NX], refs[NX : 2 * NX]
    outs, (right, total) = refs[2 * NX : 2 * NX + NY], refs[2 * NX + NY :]
    x, c, y = idx[0], idx[2], idx[3]
    half = WIDE // NC
    piece = NZ * WIDE
    for s in range(NX):
        for t in range(NZ):
            at = (x ^ s) * piece + t * WIDE
            right[pl.ds(pl.multiple_of(at + c * half, half), half), :] = mine[s][t]
            right[pl.ds(pl.multiple_of(at + (1 - c) * half, half), half), :] = other[s][t]
    for s in range(NX):
        at = slice(s * piece, (s + 1) * piece)
        part = jnp.dot(momentum[:, at], right[at, :], preferred_element_type=f32)
        total[...] = part if s == 0 else total[...] + part
    rows = total.shape[0] // NY
    for s in range(NY):
        outs[s][...] = total[pl.ds(pl.multiple_of((y ^ s) * rows, 8), rows), :]


def panel_call(idx, momentum, mine, other):
    rows, cols = momentum.shape
    rank = mine[0].shape[-1]
    return pl.pallas_call(
        panel_kernel,
        in_specs=[smem()] + [vmem()] * (1 + 2 * NX),
        out_specs=[vmem()] * NY,
        out_shape=[jax.ShapeDtypeStruct((rows // NY, rank), f32)] * NY,
        scratch_shapes=[pltpu.VMEM((cols, rank), bf16), pltpu.VMEM((rows, rank), f32)],
        compiler_params=params(),
        cost_estimate=cost(3.5),
        name="panel",
    )(idx, momentum, *mine, *other)


def tally_kernel(*refs):
    refs[-1][...] = (refs[0][...] + refs[1][...]) + (refs[2][...] + refs[3][...])


def tally_call(parts):
    return pl.pallas_call(
        tally_kernel,
        in_specs=[vmem()] * len(parts),
        out_specs=vmem(),
        out_shape=jax.ShapeDtypeStruct(parts[0].shape, f32),
        compiler_params=params(),
        cost_estimate=cost(0.7),
        name="tally",
    )(*parts)


def fold_kernel(pieces, out):
    got = pieces[0]
    for i in range(1, pieces.shape[0]):
        got = got + pieces[i]
    out[...] = got


def fold_call(pieces):
    return pl.pallas_call(
        fold_kernel,
        in_specs=[vmem()],
        out_specs=vmem(),
        out_shape=jax.ShapeDtypeStruct(pieces.shape[1:], f32),
        compiler_params=params(),
        cost_estimate=cost(0.8),
        name="fold",
    )(pieces)


def prep_kernel(idx, *refs):
    parts = refs[:NY]
    panel, pieces, gram, across = refs[NY:]
    y = idx[3]
    rows = parts[0].shape[0]
    for part, s in zip(parts, PARTNERS):
        panel[pl.ds(pl.multiple_of((y ^ s) * rows, 8), rows), :] = part[...]
    whole = panel[...]
    turned = whole.T
    rank = turned.shape[0]
    across[...] = turned
    side = rank // NY

    def product(row, count, column):
        left = across[pl.ds(pl.multiple_of(row, side // 2), count), :]
        right = across[pl.ds(pl.multiple_of(column, side), side), :]
        over = (((1,), (1,)), ((), ()))
        return lax.dot_general(left, right, over, precision=highest, preferred_element_type=f32)

    last = y == NY - 1
    below = product(jnp.where(last, y, y + 1) * side, side, jnp.where(last, 0, y) * side)
    half = product((2 + y % 2) * side + (y // 2) * (side // 2), side // 2, (y % 2) * side)
    gram[:side, :] = jnp.concatenate([product(y * side, side, y * side), below], axis=1)
    gram[side:, :] = jnp.concatenate([half[: side // 4], half[side // 4 :]], axis=1)
    for i in range(PIECES):
        now = turned.astype(bf16)
        pieces[i * rank : (i + 1) * rank, :] = now
        turned = turned - now.astype(f32)


def prep_call(idx, parts):
    rows, rank = parts[0].shape[0] * NY, parts[0].shape[1]
    return pl.pallas_call(
        prep_kernel,
        in_specs=[smem()] + [vmem()] * NY,
        out_specs=[vmem()] * 3,
        out_shape=[
            jax.ShapeDtypeStruct((rows, rank), f32),
            jax.ShapeDtypeStruct((PIECES * rank, rows), bf16),
            jax.ShapeDtypeStruct((rank // NY * 5 // 4, rank // 2), f32),
        ],
        scratch_shapes=[pltpu.VMEM((rank, rows), f32)],
        compiler_params=params(),
        cost_estimate=cost(1.5),
        name="prep",
    )(idx, *parts)


def project_kernel(part, idx, momentum, pieces, keep, send):
    x, c = idx[0], idx[2]
    rank = pieces.shape[0] // PIECES
    low = rank // 2
    first = c == 0
    wide = 2 * WIDE
    for i, s in enumerate(ORDERS[part]):
        for j in range(0, NZ // 2 * WIDE, wide):
            at = pl.multiple_of(((x ^ s) * 2 + part) * (NZ // 2 * WIDE) + j, wide)
            got = jnp.dot(pieces[...], momentum[:, pl.ds(at, wide)], preferred_element_type=f32)
            got = got[rank:] + got[:rank]
            for k in range(2):
                here = got[:, k * WIDE : (k + 1) * WIDE]
                top, bottom = here[:low], here[low:]
                keep[i, j // WIDE + k] = jnp.where(first, top, bottom)
                send[i, j // WIDE + k] = jnp.where(first, bottom, top)


def project_call(idx, momentum, pieces, part):
    rank = pieces.shape[0] // PIECES
    shape = jax.ShapeDtypeStruct((NX, NZ // 2, rank // 2, WIDE), f32)
    return pl.pallas_call(
        functools.partial(project_kernel, part),
        in_specs=[smem(), vmem(), vmem()],
        out_specs=[vmem()] * 2,
        out_shape=[shape] * 2,
        compiler_params=params(),
        cost_estimate=cost(3.5),
        name=f"project{part}",
    )(idx, momentum, pieces)


def first_kernel(keep, got, near, rest):
    for s in range(2):
        near[s] = keep[s] + got[s]
        rest[s] = keep[2 + s] + got[2 + s]


def first_call(keep, got):
    return pl.pallas_call(
        first_kernel,
        in_specs=[vmem()] * 2,
        out_specs=[vmem()] * 2,
        out_shape=[jax.ShapeDtypeStruct((2, *keep.shape[1:]), f32)] * 2,
        compiler_params=params(),
        cost_estimate=cost(0.9),
        name="first",
    )(keep, got)


def second_kernel(rest, near, own, away):
    own[...] = rest[0] + near[0]
    away[...] = rest[1] + near[1]


def second_call(rest, near):
    return pl.pallas_call(
        second_kernel,
        in_specs=[vmem()] * 2,
        out_specs=[vmem()] * 2,
        out_shape=[jax.ShapeDtypeStruct(rest.shape[1:], f32)] * 2,
        compiler_params=params(),
        cost_estimate=cost(0.9),
        name="second",
    )(rest, near)


def line_kernel(own0, near0, own1, near1, out):
    deep = own0.shape[0]
    out[:deep] = own0[...] + near0[...]
    out[deep:] = own1[...] + near1[...]


def line_call(parts):
    deep, low, wide = parts[0].shape
    return pl.pallas_call(
        line_kernel,
        in_specs=[vmem()] * len(parts),
        out_specs=vmem(),
        out_shape=jax.ShapeDtypeStruct((2 * deep, low, wide), f32),
        compiler_params=params(),
        cost_estimate=cost(0.8),
        name="line",
    )(*parts)


def share_kernel(idx, mine, other, solver, low_rank, share, turned):
    c = idx[2]
    first = c == 0
    top = jnp.where(first, mine[...], other[...])
    bottom = jnp.where(first, other[...], mine[...])
    whole = jnp.concatenate([top, bottom], axis=0)
    got = jnp.dot(solver[...], whole, precision=highest, preferred_element_type=f32)
    low = got.shape[0] // 2
    rounded = jnp.where(first, got[:low], got[low:]).astype(bf16)
    for t in range(NZ):
        low_rank[t] = rounded
    turned[...] = got.T
    half = WIDE // NC
    share[...] = turned[pl.ds(pl.multiple_of(c * half, half), half), :]


def share_call(idx, mine, other, solver):
    low, wide = mine.shape
    rank = 2 * low
    return pl.pallas_call(
        share_kernel,
        in_specs=[smem()] + [vmem()] * 3,
        out_specs=[vmem()] * 2,
        out_shape=[
            jax.ShapeDtypeStruct((NZ, low, wide), bf16),
            jax.ShapeDtypeStruct((wide // NC, rank), f32),
        ],
        scratch_shapes=[pltpu.VMEM((wide, rank), f32)],
        compiler_params=params(),
        cost_estimate=cost(1.0),
        name="share",
    )(idx, mine, other, solver)


def ortho_kernel(panel, solver, ortho):
    across = (((1,), (1,)), ((), ()))
    ortho[...] = lax.dot_general(
        panel[...], solver[...], across, precision=highest, preferred_element_type=f32
    ).astype(bf16)


def ortho_call(panel, solver):
    rows, rank = panel.shape
    return pl.pallas_call(
        ortho_kernel,
        in_specs=[vmem()] * 2,
        out_specs=vmem(),
        out_shape=jax.ShapeDtypeStruct((rows, rank), bf16),
        compiler_params=params(),
        cost_estimate=cost(0.7),
        name="ortho",
    )(panel, solver)


def square_kernel(idx, *refs):
    mine, other, out = refs[:NX], refs[NX : 2 * NX], refs[-1]
    c = idx[2]

    def total(group):
        acc = None
        for ref in group:
            for t in range(NZ):
                v = ref[t].astype(f32)
                acc = v * v if acc is None else acc + v * v
        return jnp.sum(acc, axis=1, keepdims=True)

    a, b = total(mine), total(other)
    first = c == 0
    whole = jnp.concatenate([jnp.where(first, a, b), jnp.where(first, b, a)], axis=0)
    out[...] = jnp.broadcast_to(whole, (whole.shape[0], WIDE)).T[:8]


def square_call(idx, mine, other):
    low = mine[0].shape[1]
    return pl.pallas_call(
        square_kernel,
        in_specs=[smem()] + [vmem()] * (2 * NX),
        out_specs=vmem(),
        out_shape=jax.ShapeDtypeStruct((8, 2 * low), f32),
        compiler_params=params(),
        cost_estimate=cost(1.0),
        name="square",
    )(idx, *mine, *other)


def update_kernel(idx, momentum, ortho, *refs):
    mine, other = refs[:NX], refs[NX : 2 * NX]
    out, fresh, right, sems = refs[2 * NX :]
    x, c = idx[0], idx[2]
    piece = NZ * WIDE
    low = right.shape[0] // 2
    for s in range(NX):
        for t in range(NZ):
            at = pl.ds(pl.multiple_of((x ^ s) * piece + t * WIDE, WIDE), WIDE)
            right[pl.ds(pl.multiple_of(c * low, low), low), at] = mine[s][t]
            right[pl.ds(pl.multiple_of((1 - c) * low, low), low), at] = other[s][t]
    outward = []
    for s in range(NX):
        for j in range(s * piece, (s + 1) * piece, 2 * WIDE):
            at = slice(j, j + 2 * WIDE)
            got = jnp.dot(ortho[...], right[:, at], preferred_element_type=f32)
            fresh[:, at] = (momentum[:, at].astype(f32) - feedback_rate * got).astype(bf16)
        at = pl.ds(s * piece, piece)
        outward.append(pltpu.make_async_copy(fresh.at[:, at], out.at[:, at], sems.at[s]))
        outward[-1].start()
    for copy in outward:
        copy.wait()


def update_call(idx, momentum, ortho, mine, other):
    rows, cols = momentum.shape
    rank = ortho.shape[1]
    return pl.pallas_call(
        update_kernel,
        in_specs=[smem()] + [vmem()] * (2 + 2 * NX),
        out_specs=pl.BlockSpec(memory_space=pl.ANY),
        out_shape=jax.ShapeDtypeStruct((rows, cols), bf16),
        scratch_shapes=[
            pltpu.VMEM((rows, cols), bf16),
            pltpu.VMEM((rank, cols), bf16),
            pltpu.SemaphoreType.DMA((NX,)),
        ],
        compiler_params=params(),
        cost_estimate=cost(5.0),
        name="update",
    )(idx, momentum, ortho, *mine, *other)


def invert_block(block):
    size = block.shape[0]
    strips = size // 8
    row = lax.broadcasted_iota(jnp.int32, (8, 2 * size), 0)
    eye = (
        lax.broadcasted_iota(jnp.int32, (size, size), 0)
        == lax.broadcasted_iota(jnp.int32, (size, size), 1)
    ).astype(f32)
    both = jnp.concatenate([eye, block], axis=1)
    wide = [both[8 * t : 8 * t + 8] for t in range(strips)]
    shape = (8, 2 * size)
    done = []
    for s in range(strips):
        cols = {
            t: [jnp.broadcast_to(wide[t][:, size + 8 * s + j : size + 8 * s + j + 1], shape) for j in range(8)]
            for t in range(s, strips)
        }
        scale = jnp.ones(shape, f32)
        for k in range(8):
            over = lambda v: jnp.broadcast_to(v[k : k + 1], shape)
            pivot = over(cols[s][k])
            inverse = 1.0 / pivot
            scale = jnp.where(row == k, lax.rsqrt(pivot), scale)
            lead = over(wide[s])
            heads = {j: over(cols[s][j]) for j in range(k + 1, 8)}
            for t in range(s, strips):
                factor = cols[t][k] * inverse
                if t == s:
                    factor = jnp.where(row > k, factor, 0.0)
                wide[t] = wide[t] - factor * lead
                for j in range(k + 1, 8):
                    cols[t][j] = cols[t][j] - factor * heads[j]
        done.append(wide[s] * scale)
    return jnp.concatenate(done, axis=0)[:, :size]

def solver_kernel(idx, *refs):
    parts, (out, left, right, held) = refs[:NY], refs[NY:]
    rank = out.shape[0]
    side = rank // NY
    for s in range(NY):
        held[idx[3] ^ s] = parts[s][...]
    left[...] = jnp.zeros_like(left)
    for y in range(NY):
        here = slice(y * side, (y + 1) * side)
        left[here, here] = held[y, :side, :side]
        if y == NY - 1:
            left[here, :side] = held[y, :side, side:]
        else:
            left[(y + 1) * side : (y + 2) * side, here] = held[y, :side, side:]
        row, column = (2 + y % 2) * side + y // 2 * (side // 2), (y % 2) * side
        for i in range(2):
            at = row + i * (side // 4)
            left[at : at + side // 4, column : column + side] = held[y, side:, i * side : (i + 1) * side]
    right[...] = (
        lax.broadcasted_iota(jnp.int32, (rank, rank), 0)
        == lax.broadcasted_iota(jnp.int32, (rank, rank), 1)
    ).astype(f32)
    across = (((1,), (1,)), ((), ()))
    for at in range(0, rank, BLOCK):
        end = at + BLOCK
        inverse = invert_block(left[at:end, at:end])
        rows = jnp.dot(inverse, right[at:end, :end], precision=highest, preferred_element_type=f32)
        out[at:end, :end] = rows
        if end < rank:
            out[at:end, end:] = jnp.zeros((BLOCK, rank - end), f32)
            down = lax.dot_general(left[end:, at:end], inverse, across, precision=highest, preferred_element_type=f32)
            left[end:, end:] -= lax.dot_general(down, down, across, precision=highest, preferred_element_type=f32)
            right[end:, :end] -= jnp.dot(down, rows, precision=highest, preferred_element_type=f32)

def solver_call(idx, parts):
    rank = 2 * parts[0].shape[1]
    return pl.pallas_call(
        solver_kernel,
        in_specs=[smem()] + [vmem()] * NY,
        out_specs=vmem(),
        out_shape=jax.ShapeDtypeStruct((rank, rank), f32),
        scratch_shapes=[pltpu.VMEM((rank, rank), f32)] * 2 + [pltpu.VMEM((NY, *parts[0].shape), f32)],
        compiler_params=params(),
        cost_estimate=cost(9.4),
        name="solver",
    )(idx, *parts)


def on_device(momentum, basis):
    total_cols = momentum.shape[1] * NY
    rank = basis.shape[1]
    x, z, c, y = (lax.axis_index(axis) for axis in ("x", "z", "core", "y"))
    idx = jnp.stack([x, z, c, y] + [x ^ s for order in ORDERS for s in order]).astype(jnp.int32)

    after = lax.optimization_barrier

    def stage_beside(line):
        line, late, _ = after((line, momentum, idx))
        return line, stage_call(late)

    mine, other, staged = gather_chip(spread_call(basis), stage_beside)
    parts = panel_call(idx, staged, mine, other)
    own = tally_call([parts[0]] + [flip(parts[s], "y", s) for s in (2, 1, 3)])
    panel, pieces, gram = prep_call(idx, [own] + [flip(own, "y", s) for s in PARTNERS[1:]])

    keep0, send0 = project_call(idx, staged, pieces, 0)
    got0 = other_core(send0)
    gram = gram + other_core(gram)
    gram = tally_call([gram] + [flip(gram, "x", s) for s in (1, 2, 3)])
    pieces, gram = after((pieces, gram))
    keep1, send1 = project_call(idx, staged, pieces, 1)
    got1 = other_core(send1)
    near0, rest0 = first_call(keep0, got0)
    near0 = flip(near0, "x", ORDERS[0][0])
    near1, rest1 = first_call(keep1, got1)
    near1, gram = after((near1, gram))
    near1 = flip(near1, "x", ORDERS[1][0])
    gram = tally_call([gram] + [flip(gram, "z", s) for s in (1, 2, 3)])
    rest0, gram = after((rest0, gram))
    opposite = flip(gram, "z", 4)
    own0, away0 = second_call(rest0, near0)
    away0 = flip(away0, "x", ORDERS[0][3])
    rest1, opposite = after((rest1, opposite))
    own1, away1 = second_call(rest1, near1)
    away1 = flip(away1, "x", ORDERS[1][3])
    gram = gram + opposite
    quarters = [gram] + [flip(gram, "y", s) for s in (1, 2, 3)]
    line, quarters = after((line_call([own0, away0, own1, away1]), quarters))
    sums = swap(line, "z")
    solver = solver_call(idx, quarters)
    sums, solver = after((sums, solver))
    own_sum = fold_call(sums)
    partner = other_core(own_sum)

    low_rank, share = share_call(idx, own_sum, partner, solver)

    def ortho_beside(line):
        line, staged = stage_beside(line)
        staged, late = after((staged, panel))
        return line, (staged, ortho_call(late, solver))

    mine, other, (staged, ortho) = gather_chip(low_rank, ortho_beside)
    squares = square_call(idx, mine, other)
    momentum_new = update_call(idx, staged, ortho, mine, other)
    every = squares
    for s in (1, 3, 2):
        every = every + flip(squares, "y", s)
    basis_new = share * lax.rsqrt(every[:1] / total_cols + norm_eps)
    return (momentum_new, basis_new)


def solution(mesh):
    fine = Mesh(mesh.devices.reshape(NX, NZ, NC, NY), ("x", "z", "core", "y"))
    fsdp = ("x", "z", "core")
    in_specs = (P(fsdp, "y"), P(("y", *fsdp), None))
    out_specs = (P(fsdp, "y"), P(("y", *fsdp), None))
    return jax.shard_map(
        on_device, mesh=fine, in_specs=in_specs, out_specs=out_specs, check_vma=False
    )
```
